768 devices in a mesh: col: 64 (over y, x, core), row: 12 (over z).
Axes of the slice: x: 4, y: 8, z: 12, core: 2. Of those that a mesh axis runs over, the one named last changes fastest.
Arguments:
- features: bfloat16 [196608, 512], P(('col', 'row')), may hold values from -6 to 6
- pick: int32 [768, 256], P(('col', 'row')), may hold values from 0 to 255, each once within a row
- tiles: bfloat16 [768, 12, 256, 256], P(('col', 'row')), may hold values from -0.109375 to 0.109375
- coords: int32 [768, 12, 2], P(('col', 'row')), may hold values from 0 to 11, as said below
- counts: int32 [768], P(('col', 'row')), may hold values from 1 to 12, as said below
- weight: bfloat16 [512, 512], replicated, may hold values from -0.25 to 0.25
- bias: float32 [512], replicated, may hold values from -3 to 3
- cotangent: bfloat16 [196608, 512], P(('col', 'row')), may hold values from -0.0134887695 to 0.0134887695
Outputs:
- hidden: bfloat16 [196608, 512], P(('col', 'row'))
- weight_grad: float32 [512, 512], replicated
- bias_grad: float32 [512], replicated
The draws below stay inside these ranges and needn't reach their ends.
Inputs may be any that keep to these rules, and one draw needn't show every extreme that they name: `coords`: entry 0 of slot t is (t + k) mod 12 for a number k of each device; entry 1 is any block of the column. `counts`: all 12 devices of one column hold 12 live tiles.
All inputs are finite; a program needn't handle non-finite values.
Results may differ from the reference program's by a relative error of at most 0.0075.
Values may be sent and summed in bfloat16 or wider, within the bound.
No kernel may reach another device: no remote copies, remote signals or barrier semaphores. Data moves between devices by JAX's collectives and lax.ppermute only.
A program may use at most 64 MiB of HBM per device.

```python
import jax
import jax.numpy as jnp
from jax import lax

BS = 256
F = 512
TILE_MAX = 12
BLOCKS = 768
NODES = 196608
N_COL = 64
N_ROW = 12


def draw_coords(key, part):
    key = jax.random.fold_in(key, 11)
    first, second = jax.random.split(key)
    offset = jax.random.randint(first, (BLOCKS, 1), 0, N_ROW)
    slots = jnp.arange(TILE_MAX, dtype=jnp.int32)[None, :]
    outer = (slots + offset) % N_ROW
    inner = jax.random.randint(second, (BLOCKS, TILE_MAX), 0, N_ROW)
    return jnp.stack([outer, inner], axis=-1).astype(jnp.int32)


def draw_counts(key, part):
    key = jax.random.fold_in(key, 23)
    first, second = jax.random.split(key)
    drawn = jax.random.randint(first, (BLOCKS,), 1, TILE_MAX + 1)
    full_column = jax.random.randint(second, (), 0, N_COL)
    column = jnp.arange(BLOCKS, dtype=jnp.int32) // N_ROW
    return jnp.where(column == full_column, TILE_MAX, drawn).astype(jnp.int32)


def levels(rng, shape, cuts, least, top_value):
    factor_of = 1.0
    for position, parts in cuts:
        draws = jax.random.uniform(jax.random.fold_in(jax.random.fold_in(rng, 6), position), (parts,), jnp.float32, least / len(cuts), top_value / len(cuts))
        factor_of = factor_of * jnp.repeat(jnp.exp(draws), shape[position] // parts).reshape((-1,) + (1,) * (len(shape) - 1 - position))
    return factor_of


def noise(key, extent, width, reach, cuts=(), held_as=jnp.bfloat16):
    loudness = levels(key, extent, cuts, -0.22, 0.18) if cuts else 1.0
    array = jax.random.normal(key, extent, jnp.float32) * width * loudness
    return jnp.minimum(jnp.maximum(array, -reach), reach).astype(held_as)


def setup_inputs(seed: int = 0) -> dict:
    seeds = jax.random.split(jax.random.key(seed), 9)
    return {
        "features": noise(seeds[0], (NODES, F), 1.0, 6.0, ((0, 768),)),
        "pick": jax.vmap(lambda own: jax.random.permutation(own, BS))(jax.random.split(seeds[1], BLOCKS)).reshape((BLOCKS, BS)).astype(jnp.int32),
        "tiles": noise(seeds[2], (BLOCKS, TILE_MAX, BS, BS), (BS * TILE_MAX) ** -0.5, 0.109375, ((0, 768),)),
        "coords": draw_coords(jax.random.fold_in(seeds[8], 71), 0),
        "counts": draw_counts(jax.random.fold_in(seeds[8], 71), 0),
        "weight": noise(seeds[5], (F, F), F ** -0.5, 0.25),
        "bias": noise(seeds[6], (F,), 0.5, 3.0, (), jnp.float32),
        "cotangent": noise(seeds[7], (NODES, F), (1.0 / NODES ** 0.5), 0.0134887695, ((0, 768),)),
    }


def column_sums(blocks, tile_set, coord_set, live_set):
    inputs = blocks[coord_set[:, :, 1]].astype(jnp.float32)
    products = jnp.einsum("rtab,rtbf->rtaf", tile_set.astype(jnp.float32), inputs)
    owners = jnp.arange(N_ROW, dtype=jnp.int32)
    select = ((coord_set[:, :, 0][:, :, None] == owners) & live_set[:, :, None]).astype(jnp.float32)
    return jnp.einsum("rto,rtaf->oaf", select, products, precision=lax.Precision.HIGHEST)


def reference(features, pick, tiles, coords, counts, weight, bias, cotangent):
    slot_rows = BS // N_COL
    viewed = features.reshape(N_COL, N_ROW, BS, F)
    orders = pick.reshape(N_COL, N_ROW, BS).astype(jnp.int32)
    chosen = jax.vmap(jax.vmap(lambda block, order: block[order]))(viewed, orders)
    chosen = chosen.reshape(N_COL, N_ROW, N_COL, slot_rows, F)
    blocked = jnp.transpose(chosen, (2, 1, 0, 3, 4)).reshape(N_COL, N_ROW, BS, F)
    tile_grid = tiles.reshape(N_COL, N_ROW, TILE_MAX, BS, BS)
    coord_grid = coords.reshape(N_COL, N_ROW, TILE_MAX, 2).astype(jnp.int32)
    live_grid = jnp.arange(TILE_MAX, dtype=jnp.int32)[None, None, :] < counts.reshape(N_COL, N_ROW)[:, :, None]
    sums = lax.map(lambda packed: column_sums(*packed), (blocked, tile_grid, coord_grid, live_grid))
    aggregated = sums.astype(jnp.bfloat16).reshape(NODES, F)
    pre = jnp.dot(aggregated, weight, preferred_element_type=jnp.float32) + bias.astype(jnp.float32)
    sigmoid_v = jax.nn.sigmoid(pre)
    hidden = (pre * sigmoid_v).astype(jnp.bfloat16)
    grad_pre = (cotangent.astype(jnp.float32) * sigmoid_v * (1.0 + pre * (1.0 - sigmoid_v))).astype(jnp.bfloat16)
    weight_grad = jnp.dot(aggregated.T, grad_pre, preferred_element_type=jnp.float32)
    bias_grad = jnp.sum(grad_pre.astype(jnp.float32), axis=0)
    return hidden, weight_grad, bias_grad
```

```python
import functools

import jax
import jax.numpy as jnp
from jax import lax
from jax.experimental import pallas as pl
from jax.experimental.pallas import tpu as pltpu
from jax.sharding import PartitionSpec as P

BF16 = jnp.bfloat16
F32 = jnp.float32
LANES = 128
META_ROWS = 8
VMEM_LIMIT = 40 * 1024 * 1024
IN_VMEM = pl.BlockSpec(memory_space=pltpu.VMEM)
IN_SMEM = pl.BlockSpec(memory_space=pltpu.SMEM)
IN_PLACE = pl.BlockSpec(memory_space=pl.ANY)
PARAMS = pltpu.CompilerParams(vmem_limit_bytes=VMEM_LIMIT)


def order_tiles(first, tile_set):
    n = tile_set.shape[0]

    def kernel(first_ref, tiles_ref, out_ref, sems):
        copies = []
        for o in range(n):
            slot = lax.rem(o + n - first_ref[0], n)
            copies.append(pltpu.make_async_copy(tiles_ref.at[slot], out_ref.at[o], sems.at[o]))
            copies[-1].start()
        for copy in copies:
            copy.wait()

    return pl.pallas_call(
        kernel,
        out_shape=jax.ShapeDtypeStruct(tile_set.shape, tile_set.dtype),
        in_specs=[IN_SMEM, IN_PLACE],
        out_specs=IN_PLACE,
        scratch_shapes=[pltpu.SemaphoreType.DMA((n,))],
        compiler_params=PARAMS,
        cost_estimate=pl.CostEstimate(
            flops=0, bytes_accessed=2 * tile_set.size * 2, transcendentals=0
        ),
    )(first, tile_set)


def layer(which, tiles, blocks, weight, bias, cotangent):
    n, rows, _ = tiles.shape
    width = weight.shape[0]

    def kernel(which_ref, tiles_ref, blocks_ref, weight_ref, bias_ref, cot_ref, hidden_ref, grad_ref):
        total = jnp.zeros((rows, width), F32)
        for s in range(n):
            index = which_ref[s]
            live = (index >= 0).astype(F32).astype(BF16)
            block = blocks_ref[jnp.maximum(index, 0), :rows, :]
            total = total + jnp.dot(tiles_ref[s] * live, block, preferred_element_type=F32)
        aggregated = total.astype(BF16)
        pre = jnp.dot(aggregated, weight_ref[...], preferred_element_type=F32) + bias_ref[...]
        sig = jax.nn.sigmoid(pre)
        hidden_ref[...] = (pre * sig).astype(BF16)
        grad_pre = (cot_ref[...].astype(F32) * sig * (1.0 + pre * (1.0 - sig))).astype(BF16)
        over_nodes = (((0,), (0,)), ((), ()))
        grad_ref[:, :width] = lax.dot_general(
            aggregated, grad_pre, over_nodes, preferred_element_type=F32
        ).astype(BF16)
        ones = jnp.ones((rows, LANES), BF16)
        column = lax.dot_general(grad_pre, ones, over_nodes, preferred_element_type=F32)
        high = column.astype(BF16)
        low = (column - high.astype(F32)).astype(BF16)
        lane = lax.broadcasted_iota(jnp.int32, column.shape, 1)
        grad_ref[:, width:] = jnp.where(lane < LANES // 2, high.astype(F32), low.astype(F32)).astype(BF16)

    return pl.pallas_call(
        kernel,
        out_shape=(
            jax.ShapeDtypeStruct((rows, width), BF16),
            jax.ShapeDtypeStruct((width, width + LANES), BF16),
        ),
        in_specs=[IN_SMEM] + [IN_VMEM] * 5,
        out_specs=(IN_VMEM, IN_VMEM),
        compiler_params=PARAMS,
        cost_estimate=pl.CostEstimate(
            flops=2 * rows * width * (n * rows + 2 * width),
            bytes_accessed=6 * 1024 * 1024,
            transcendentals=rows * width,
        ),
    )(which, tiles, blocks, weight, bias, cotangent)


def sum_over_col(parts, copies):
    n, rows, wide = parts.shape

    def kernel(parts_ref, out_ref):
        total = parts_ref[0].astype(F32)
        for i in range(1, n):
            total = total + parts_ref[i].astype(F32)
        for i in range(copies):
            out_ref[i] = total

    return pl.pallas_call(
        kernel,
        out_shape=jax.ShapeDtypeStruct((copies, rows, wide), F32),
        in_specs=[IN_VMEM],
        out_specs=IN_VMEM,
        compiler_params=PARAMS,
    )(parts)


def sum_over_row(place, parts, copies, width):
    n, rows, wide = parts.shape

    def kernel(place_ref, parts_ref, out_ref):
        total = parts_ref[0]
        for i in range(1, n):
            total = total + parts_ref[i]
        column = total[:, width : width + 1] + total[:, width + LANES // 2 : width + LANES // 2 + 1]
        lane = lax.broadcasted_iota(jnp.int32, (rows, LANES), 1)
        row = lax.broadcasted_iota(jnp.int32, (rows, LANES), 0)
        mine = lane == lax.rem(place_ref[0] * rows, LANES) + row
        line = jnp.sum(jnp.where(mine, column, 0.0), axis=0, keepdims=True)
        high = line.astype(BF16).astype(F32)
        tail = jnp.where(row == 0, high, jnp.where(row == 1, line - high, 0.0)).astype(BF16)
        weights = total[:, :width].astype(BF16)
        for i in range(copies):
            out_ref[i, :, :width] = weights
            out_ref[i, :, width:] = tail

    return pl.pallas_call(
        kernel,
        out_shape=jax.ShapeDtypeStruct((copies, rows, wide), BF16),
        in_specs=[IN_SMEM, IN_VMEM],
        out_specs=IN_VMEM,
        compiler_params=PARAMS,
    )(place, parts)


def unpack(parts, width):
    n, rows, wide = parts.shape
    per_group = LANES // rows

    def kernel(parts_ref, weight_ref, bias_ref):
        for i in range(n):
            weight_ref[i * rows : (i + 1) * rows, :] = parts_ref[i, :, :width].astype(F32)
        for g in range(n // per_group):
            line = parts_ref[g * per_group, :, width:].astype(F32)
            for i in range(1, per_group):
                line = line + parts_ref[g * per_group + i, :, width:].astype(F32)
            bias_ref[:, g * LANES : (g + 1) * LANES] = jnp.sum(line, axis=0, keepdims=True)

    return pl.pallas_call(
        kernel,
        out_shape=(
            jax.ShapeDtypeStruct((n * rows, width), F32),
            jax.ShapeDtypeStruct((1, n * rows), F32),
        ),
        in_specs=[IN_VMEM],
        out_specs=(IN_VMEM, IN_VMEM),
        compiler_params=PARAMS,
    )(parts)


def on_device(features, pick, tiles, coords, counts, weight, bias, cotangent):
    col_count = lax.axis_size("col")
    row_count = lax.axis_size("row")
    block_rows, width = features.shape
    slot_rows = block_rows // col_count
    exchange = functools.partial(lax.all_to_all, split_axis=0, concat_axis=0, tiled=True)

    sent = features[pick[0]].reshape(col_count, slot_rows, width)
    blocked = exchange(sent, "col").reshape(block_rows, width)

    first = coords[0, :1, 0]
    slots = lax.rem(jnp.arange(row_count, dtype=jnp.int32) + row_count - first, row_count)
    inputs = jnp.where(slots < counts[0], coords[0, slots, 1], -1)
    meta = jnp.zeros((META_ROWS, width), BF16).at[0, :row_count].set(inputs.astype(BF16))
    whole = lax.all_gather(jnp.concatenate([blocked, meta], axis=0), "row", axis=0, tiled=True)
    whole = whole.reshape(row_count, block_rows + META_ROWS, width)

    ordered = order_tiles(first, tiles[0])
    ordered, _ = lax.optimization_barrier((ordered, blocked))
    mine = exchange(ordered, "row")

    me = lax.axis_index("row")
    which = lax.dynamic_index_in_dim(whole[:, block_rows, :row_count], me, 1, keepdims=False)
    hidden, grads = layer(
        which.astype(jnp.int32), mine, whole, weight, bias.reshape(1, width), cotangent
    )

    grad_rows = width // col_count
    parts = exchange(grads.reshape(col_count, grad_rows, width + LANES), "col")
    parts = exchange(sum_over_col(parts, row_count), "row")
    place = lax.axis_index("col").astype(jnp.int32).reshape(1)
    parts = exchange(sum_over_row(place, parts, col_count, width), "col")
    weight_grad, bias_grad = unpack(parts, width)
    return hidden, weight_grad, bias_grad.reshape(width)


def solution(mesh):
    in_specs = (
        P(("col", "row"), None),
        P(("col", "row"), None),
        P(("col", "row"), None, None, None),
        P(("col", "row"), None, None),
        P(("col", "row")),
        P(),
        P(),
        P(("col", "row"), None),
    )
    out_specs = (P(("col", "row"), None), P(), P())
    return jax.shard_map(
        on_device, mesh=mesh, in_specs=in_specs, out_specs=out_specs, check_vma=False
    )
```

```python
import functools

import jax
import jax.numpy as jnp
from jax import lax
from jax.experimental import pallas as pl
from jax.experimental.pallas import tpu as pltpu
from jax.sharding import PartitionSpec as P

BF16 = jnp.bfloat16
F32 = jnp.float32
LANES = 128
META_ROWS = 16
STRIDE = 4
STRIDE = 4
ROUTES = ((0, 0, 2), (1, 0, 2), (-1, 0, 2), (2, 0, 1), (-2, 1, 2))
VMEM_LIMIT = 16 * 1024 * 1024
IN_VMEM = pl.BlockSpec(memory_space=pltpu.VMEM)
IN_SMEM = pl.BlockSpec(memory_space=pltpu.SMEM)
IN_PLACE = pl.BlockSpec(memory_space=pl.ANY)
PARAMS = pltpu.CompilerParams(vmem_limit_bytes=VMEM_LIMIT)


def bundle_tiles(place, count, coords, tile_set):
    n, rows, columns = tile_set.shape
    size, half = n // STRIDE, rows // 2
    heights = [(last - begin) * half for _, begin, last in ROUTES]
    pieces = len(heights) * size

    def kernel(place_ref, count_ref, coords_ref, tiles_ref, *refs):
        out_refs, (meta, tile_sems, meta_sems) = refs[: len(heights)], refs[len(heights) :]
        here, turn, first = place_ref[0], place_ref[1], coords_ref[0]
        copies = []
        for g, (behind, begin, _) in enumerate(ROUTES):
            for p in range(size):
                i = g * size + p
                output = here + turn * (p * STRIDE - behind)
                slot = lax.rem(output - first + 3 * n, n)
                source = tiles_ref.at[slot, pl.ds(begin * half, heights[g])]
                target = out_refs[g].at[p, pl.ds(0, heights[g])]
                copies.append(pltpu.make_async_copy(source, target, tile_sems.at[i]))
                copies[-1].start()
                block = jnp.where(slot < count_ref[0], coords_ref[2 * slot + 1], -1)
                meta[i] = jnp.full(meta.shape[1:], block.astype(F32), F32).astype(BF16)
                note = out_refs[g].at[p, pl.ds(heights[g], META_ROWS)]
                copies.append(pltpu.make_async_copy(meta.at[i], note, meta_sems.at[i]))
                copies[-1].start()
        for copy in copies:
            copy.wait()

    return pl.pallas_call(
        kernel,
        out_shape=[
            jax.ShapeDtypeStruct((size, height + META_ROWS, columns), tile_set.dtype)
            for height in heights
        ],
        in_specs=[IN_SMEM] * 3 + [IN_PLACE],
        out_specs=[IN_PLACE] * len(heights),
        scratch_shapes=[
            pltpu.VMEM((pieces, META_ROWS, columns), tile_set.dtype),
            pltpu.SemaphoreType.DMA((pieces,)),
            pltpu.SemaphoreType.DMA((pieces,)),
        ],
        compiler_params=PARAMS,
        cost_estimate=pl.CostEstimate(
            flops=0, bytes_accessed=2 * tile_set.size * 2, transcendentals=0
        ),
    )(place, count, coords, tile_set)


def partial_sums(bundles, blocks):
    groups, size = len(bundles), bundles[0].shape[0]
    n, rows, width = blocks.shape
    half = rows // 2

    def kernel(*refs):
        bundle_refs, blocks_ref = refs[:groups], refs[groups]
        out_refs, sums = refs[groups + 1 : -1], refs[-1]
        sums[...] = jnp.zeros_like(sums)
        for p in range(size):
            for bundle_ref, (_, begin, last) in zip(bundle_refs, ROUTES):
                height = (last - begin) * half
                note = bundle_ref[p, height : height + META_ROWS, :LANES].astype(F32)
                block = jnp.max(note).astype(jnp.int32)

                @pl.when(block >= 0)
                def _():
                    sums[p, begin * half : last * half, :] += jnp.dot(
                        bundle_ref[p, :height, :], blocks_ref[block], preferred_element_type=F32
                    )

        for p, out_ref in enumerate(out_refs):
            out_ref[...] = sums[p].astype(out_ref.dtype)

    return pl.pallas_call(
        kernel,
        out_shape=[
            jax.ShapeDtypeStruct((rows, width), F32 if p == 0 else BF16) for p in range(size)
        ],
        in_specs=[IN_VMEM] * (groups + 1),
        out_specs=[IN_VMEM] * size,
        scratch_shapes=[pltpu.VMEM((size, rows, width), F32)],
        compiler_params=PARAMS,
        cost_estimate=pl.CostEstimate(
            flops=2 * n * rows * rows * width,
            bytes_accessed=6 * 1024 * 1024,
            transcendentals=0,
        ),
    )(*bundles, blocks)


def layer(core, sums, weight, bias, cotangent):
    rows, width = cotangent.shape
    parts, half = len(sums), width // 2

    def kernel(core_ref, *refs):
        sum_refs = refs[:parts]
        weight_ref, bias_ref, cot_ref, hidden_ref, keep_ref, give_ref = refs[parts:]
        total = sum_refs[0][...].astype(F32)
        for sum_ref in sum_refs[1:]:
            total = total + sum_ref[...].astype(F32)
        aggregated = total.astype(BF16)
        pre = jnp.dot(aggregated, weight_ref[...], preferred_element_type=F32) + bias_ref[...]
        sig = jax.nn.sigmoid(pre)
        hidden_ref[...] = (pre * sig).astype(BF16)
        grad_pre = (cot_ref[...].astype(F32) * sig * (1.0 + pre * (1.0 - sig))).astype(BF16)
        over_nodes = (((0,), (0,)), ((), ()))
        ones = jnp.ones((rows, LANES), BF16)
        first = core_ref[0] == 0
        for out_ref, low in ((keep_ref, first), (give_ref, jnp.logical_not(first))):
            left = jnp.where(low, aggregated[:, :half], aggregated[:, half:])
            out_ref[:, :width] = lax.dot_general(
                left, grad_pre, over_nodes, preferred_element_type=F32
            ).astype(BF16)
            left = jnp.where(low, grad_pre[:, :half], grad_pre[:, half:])
            out_ref[:, width:] = lax.dot_general(
                left, ones, over_nodes, preferred_element_type=F32
            ).astype(BF16)

    gradient = jax.ShapeDtypeStruct((half, width + LANES), BF16)
    return pl.pallas_call(
        kernel,
        out_shape=(jax.ShapeDtypeStruct((rows, width), BF16), gradient, gradient),
        in_specs=[IN_SMEM] + [IN_VMEM] * (parts + 3),
        out_specs=(IN_VMEM, IN_VMEM, IN_VMEM),
        compiler_params=PARAMS,
        cost_estimate=pl.CostEstimate(
            flops=4 * rows * width * width,
            bytes_accessed=3 * 1024 * 1024,
            transcendentals=rows * width,
        ),
    )(core, *sums, weight, bias, cotangent)


def sum_two(left, right):
    def kernel(left_ref, right_ref, out_ref):
        out_ref[...] = (left_ref[...].astype(F32) + right_ref[...].astype(F32)).astype(BF16)

    return pl.pallas_call(
        kernel,
        out_shape=jax.ShapeDtypeStruct(left.shape, BF16),
        in_specs=[IN_VMEM] * 2,
        out_specs=IN_VMEM,
        compiler_params=PARAMS,
    )(left, right)


def sum_over_chips(parts, copies):
    n, rows, wide = parts.shape

    def kernel(parts_ref, out_ref):
        total = parts_ref[0].astype(F32)
        for i in range(1, n):
            total = total + parts_ref[i].astype(F32)
        packed = total.astype(BF16)
        for i in range(copies):
            out_ref[i] = packed

    return pl.pallas_call(
        kernel,
        out_shape=jax.ShapeDtypeStruct((copies, rows, wide), BF16),
        in_specs=[IN_VMEM],
        out_specs=IN_VMEM,
        compiler_params=PARAMS,
    )(parts)


def sum_over_row(chip, parts, copies, width):
    n, rows, wide = parts.shape

    def kernel(chip_ref, parts_ref, out_ref):
        total = parts_ref[0].astype(F32)
        for i in range(1, n):
            total = total + parts_ref[i].astype(F32)
        lane = lax.broadcasted_iota(jnp.int32, (rows, LANES), 1)
        row = lax.broadcasted_iota(jnp.int32, (rows, LANES), 0)
        mine = lane == lax.rem(chip_ref[0] * rows, LANES) + row
        tail = jnp.where(mine, total[:, width:], 0.0).astype(BF16)
        weights = total[:, :width].astype(BF16)
        for i in range(copies):
            out_ref[i, :, :width] = weights
            out_ref[i, :, width:] = tail

    return pl.pallas_call(
        kernel,
        out_shape=jax.ShapeDtypeStruct((copies, rows, wide), BF16),
        in_specs=[IN_SMEM, IN_VMEM],
        out_specs=IN_VMEM,
        compiler_params=PARAMS,
    )(chip, parts)


def unpack(core, mine, other, width):
    n, rows, wide = mine.shape
    per_group = LANES // rows
    half = n * rows

    def kernel(core_ref, mine_ref, other_ref, weight_ref, bias_ref):
        for parts_ref, at in ((mine_ref, core_ref[0]), (other_ref, 1 - core_ref[0])):
            base = pl.multiple_of(at * half, half)
            for i in range(n):
                weight_ref[pl.ds(base + i * rows, rows), :] = parts_ref[i, :, :width].astype(F32)
            for g in range(n // per_group):
                line = parts_ref[g * per_group, :, width:].astype(F32)
                for i in range(1, per_group):
                    line = line + parts_ref[g * per_group + i, :, width:].astype(F32)
                line = jnp.sum(line, axis=0, keepdims=True)
                bias_ref[:, pl.ds(pl.multiple_of(base + g * LANES, LANES), LANES)] = line

    return pl.pallas_call(
        kernel,
        out_shape=(
            jax.ShapeDtypeStruct((2 * half, width), F32),
            jax.ShapeDtypeStruct((1, 2 * half), F32),
        ),
        in_specs=[IN_SMEM, IN_VMEM, IN_VMEM],
        out_specs=(IN_VMEM, IN_VMEM),
        compiler_params=PARAMS,
    )(core, mine, other)


def on_device(features, pick, tiles, coords, counts, weight, bias, cotangent):
    col_count = lax.axis_size("col")
    row_count = lax.axis_size("row")
    block_rows, width = features.shape
    slot_rows = block_rows // col_count
    exchange = functools.partial(lax.all_to_all, split_axis=0, concat_axis=0, tiled=True)

    def permute(x, step):
        pairs = []
        for col in range(col_count):
            turn = 1 - 2 * (col % 2)
            for row in range(row_count):
                target = (row + turn * step(turn * row % row_count)) % row_count
                pairs.append((col * row_count + row, col * row_count + target))
        return lax.ppermute(x, ("col", "row"), pairs)

    col, row = (lax.axis_index(axis).astype(jnp.int32) for axis in ("col", "row"))
    place = jnp.stack([row, 1 - 2 * lax.rem(col, 2)])

    sent = features[pick[0]].reshape(col_count, slot_rows, width)
    blocked = exchange(sent, "col").reshape(block_rows, width)
    blocks = lax.all_gather(blocked, "row", axis=0)

    bundles = bundle_tiles(place, counts, coords.reshape(-1), tiles[0])
    bundles = [
        permute(x, lambda _, behind=route[0]: -behind) if route[0] else x
        for x, route in zip(bundles, ROUTES)
    ]
    sums = partial_sums(bundles, blocks)
    sums = [sums[0]] + [permute(sums[p], lambda _, p=p: p * STRIDE) for p in range(1, len(sums))]
    core = lax.rem(col, 2).reshape(1)
    hidden, keep, give = layer(core, sums, weight, bias.reshape(1, width), cotangent)

    chips = col_count // 2
    cores = [[2 * chip + k for chip in range(chips)] for k in range(2)]
    other_core = [(i, i ^ 1) for i in range(col_count)]
    parts = sum_two(keep, lax.ppermute(give, "col", other_core))
    parts = parts.reshape(chips, width // col_count, width + LANES)
    parts = exchange(parts, "col", axis_index_groups=cores)
    parts = exchange(sum_over_chips(parts, row_count), "row")
    parts = sum_over_row(lax.div(col, 2).reshape(1), parts, chips, width)
    mine = exchange(parts, "col", axis_index_groups=cores)
    other = lax.ppermute(mine, "col", other_core)
    weight_grad, bias_grad = unpack(core, mine, other, width)
    return hidden, weight_grad, bias_grad.reshape(width)


def solution(mesh):
    in_specs = (
        P(("col", "row"), None),
        P(("col", "row"), None),
        P(("col", "row"), None, None, None),
        P(("col", "row"), None, None),
        P(("col", "row")),
        P(),
        P(),
        P(("col", "row"), None),
    )
    out_specs = (P(("col", "row"), None), P(), P())
    return jax.shard_map(
        on_device, mesh=mesh, in_specs=in_specs, out_specs=out_specs, check_vma=False
    )
```

```python
import functools

import jax
import jax.numpy as jnp
from jax import lax
from jax.experimental import pallas as pl
from jax.experimental.pallas import tpu as pltpu
from jax.sharding import PartitionSpec as P

BF16 = jnp.bfloat16
F32 = jnp.float32
LANES = 128
META_ROWS = 16
STRIDE = 4
TIE = 1
VMEM_LIMIT = 16 * 1024 * 1024
IN_VMEM = pl.BlockSpec(memory_space=pltpu.VMEM)
IN_SMEM = pl.BlockSpec(memory_space=pltpu.SMEM)
IN_PLACE = pl.BlockSpec(memory_space=pl.ANY)
PARAMS = pltpu.CompilerParams(vmem_limit_bytes=VMEM_LIMIT)


def ring_place(place_ref, n):
    here, turn = place_ref[0], place_ref[1]
    near = jnp.where(lax.rem(here, 2) == 0, 1, -1)
    far = jnp.where(lax.rem(lax.div(lax.rem(here * turn + n, n), 2), 2) == 0, 1, -1)
    return here, turn, near, far


def routes(near, far):
    return (0, near, -near, 2 * far)


def bundle_tiles(place, count, coords, tile_set):
    n, rows, columns = tile_set.shape
    size = n // STRIDE

    def kernel(place_ref, count_ref, coords_ref, tiles_ref, *refs):
        out_refs, (meta, tile_sems, meta_sems) = refs[:STRIDE], refs[STRIDE:]
        here, turn, near, far = ring_place(place_ref, n)
        first = coords_ref[0]
        copies = []
        for g, ahead in enumerate(routes(near, far)):
            for p in range(size):
                i = g * size + p
                output = here + turn * (p * STRIDE + ahead)
                slot = lax.rem(output - first + 3 * n, n)
                target = out_refs[g].at[p, pl.ds(0, rows)]
                copies.append(pltpu.make_async_copy(tiles_ref.at[slot], target, tile_sems.at[i]))
                copies[-1].start()
                block = jnp.where(slot < count_ref[0], coords_ref[2 * slot + 1], -1)
                meta[i] = jnp.full(meta.shape[1:], block.astype(F32), F32).astype(BF16)
                note = out_refs[g].at[p, pl.ds(rows, META_ROWS)]
                copies.append(pltpu.make_async_copy(meta.at[i], note, meta_sems.at[i]))
                copies[-1].start()
        for copy in copies:
            copy.wait()

    bundle = jax.ShapeDtypeStruct((size, rows + META_ROWS, columns), tile_set.dtype)
    return pl.pallas_call(
        kernel,
        out_shape=[bundle] * STRIDE,
        in_specs=[IN_SMEM] * 3 + [IN_PLACE],
        out_specs=[IN_PLACE] * STRIDE,
        scratch_shapes=[
            pltpu.VMEM((n, META_ROWS, columns), tile_set.dtype),
            pltpu.SemaphoreType.DMA((n,)),
            pltpu.SemaphoreType.DMA((n,)),
        ],
        compiler_params=PARAMS,
        cost_estimate=pl.CostEstimate(
            flops=0, bytes_accessed=2 * tile_set.size * 2, transcendentals=0
        ),
    )(place, count, coords, tile_set)


def partial_sums(place, bundles, blocks):
    groups, size = len(bundles), bundles[0].shape[0]
    n = len(blocks)
    rows, width = blocks[0].shape

    def kernel(place_ref, *refs):
        bundle_refs = refs[:groups]
        block_refs = refs[groups : groups + n]
        out_refs = refs[groups + n : -2]
        sums, which = refs[-2:]
        here, turn, near, _ = ring_place(place_ref, n)
        for g, bundle_ref in enumerate(bundle_refs):
            for p in range(size):
                note = bundle_ref[p, rows : rows + META_ROWS, :LANES].astype(F32)
                block = jnp.max(note).astype(jnp.int32)
                away = lax.rem(near * turn * (block - here) + n, n)
                which[g * size + p] = jnp.where(block < 0, -1, away)
        sums[...] = jnp.zeros_like(sums)
        for d, block_ref in enumerate(block_refs):
            for g, bundle_ref in enumerate(bundle_refs):

                @pl.loop(0, size)
                def _(p):
                    @pl.when(which[g * size + p] == d)
                    def _():
                        sums[p] += jnp.dot(
                            bundle_ref[p, :rows, :], block_ref[...], preferred_element_type=F32
                        )

        for p, out_ref in enumerate(out_refs):
            out_ref[...] = sums[p].astype(out_ref.dtype)

    return pl.pallas_call(
        kernel,
        out_shape=[
            jax.ShapeDtypeStruct((rows, width), F32 if p == 0 else BF16) for p in range(size)
        ],
        in_specs=[IN_SMEM] + [IN_VMEM] * (groups + n),
        out_specs=[IN_VMEM] * size,
        scratch_shapes=[
            pltpu.VMEM((size, rows, width), F32),
            pltpu.SMEM((groups * size,), jnp.int32),
        ],
        compiler_params=PARAMS,
        cost_estimate=pl.CostEstimate(
            flops=2 * n * rows * rows * width,
            bytes_accessed=6 * 1024 * 1024,
            transcendentals=0,
        ),
    )(place, *bundles, *blocks)


def layer(core, sums, weight, bias, cotangent):
    rows, width = cotangent.shape
    parts, half = len(sums), width // 2

    def kernel(core_ref, *refs):
        sum_refs = refs[:parts]
        weight_ref, bias_ref, cot_ref, hidden_ref, keep_ref, give_ref = refs[parts:]
        total = sum_refs[0][...].astype(F32)
        for sum_ref in sum_refs[1:]:
            total = total + sum_ref[...].astype(F32)
        aggregated = total.astype(BF16)
        pre = jnp.dot(aggregated, weight_ref[...], preferred_element_type=F32) + bias_ref[...]
        sig = jax.nn.sigmoid(pre)
        hidden_ref[...] = (pre * sig).astype(BF16)
        grad_pre = (cot_ref[...].astype(F32) * sig * (1.0 + pre * (1.0 - sig))).astype(BF16)
        over_nodes = (((0,), (0,)), ((), ()))
        ones = jnp.ones((rows, LANES), BF16)
        first = core_ref[0] == 0
        for out_ref, low in ((keep_ref, first), (give_ref, jnp.logical_not(first))):
            left = jnp.where(low, aggregated[:, :half], aggregated[:, half:])
            out_ref[:, :width] = lax.dot_general(
                left, grad_pre, over_nodes, preferred_element_type=F32
            ).astype(BF16)
            left = jnp.where(low, grad_pre[:, :half], grad_pre[:, half:])
            out_ref[:, width:] = lax.dot_general(
                left, ones, over_nodes, preferred_element_type=F32
            ).astype(BF16)

    gradient = jax.ShapeDtypeStruct((half, width + LANES), BF16)
    return pl.pallas_call(
        kernel,
        out_shape=(jax.ShapeDtypeStruct((rows, width), BF16), gradient, gradient),
        in_specs=[IN_SMEM] + [IN_VMEM] * (parts + 3),
        out_specs=(IN_VMEM, IN_VMEM, IN_VMEM),
        compiler_params=PARAMS,
        cost_estimate=pl.CostEstimate(
            flops=4 * rows * width * width,
            bytes_accessed=3 * 1024 * 1024,
            transcendentals=rows * width,
        ),
    )(core, *sums, weight, bias, cotangent)


def sum_two(left, right):
    def kernel(left_ref, right_ref, out_ref):
        out_ref[...] = (left_ref[...].astype(F32) + right_ref[...].astype(F32)).astype(BF16)

    return pl.pallas_call(
        kernel,
        out_shape=jax.ShapeDtypeStruct(left.shape, BF16),
        in_specs=[IN_VMEM] * 2,
        out_specs=IN_VMEM,
        compiler_params=PARAMS,
    )(left, right)


def sum_over_chips(parts, copies):
    n, rows, wide = parts.shape

    def kernel(parts_ref, out_ref):
        total = parts_ref[0].astype(F32)
        for i in range(1, n):
            total = total + parts_ref[i].astype(F32)
        packed = total.astype(BF16)
        for i in range(copies):
            out_ref[i] = packed

    return pl.pallas_call(
        kernel,
        out_shape=jax.ShapeDtypeStruct((copies, rows, wide), BF16),
        in_specs=[IN_VMEM],
        out_specs=IN_VMEM,
        compiler_params=PARAMS,
    )(parts)


def sum_over_row(chip, parts, copies, width):
    n, rows, wide = parts.shape

    def kernel(chip_ref, parts_ref, out_ref):
        total = parts_ref[0].astype(F32)
        for i in range(1, n):
            total = total + parts_ref[i].astype(F32)
        lane = lax.broadcasted_iota(jnp.int32, (rows, LANES), 1)
        row = lax.broadcasted_iota(jnp.int32, (rows, LANES), 0)
        mine = lane == lax.rem(chip_ref[0] * rows, LANES) + row
        tail = jnp.where(mine, total[:, width:], 0.0).astype(BF16)
        weights = total[:, :width].astype(BF16)
        for i in range(copies):
            out_ref[i, :, :width] = weights
            out_ref[i, :, width:] = tail

    return pl.pallas_call(
        kernel,
        out_shape=jax.ShapeDtypeStruct((copies, rows, wide), BF16),
        in_specs=[IN_SMEM, IN_VMEM],
        out_specs=IN_VMEM,
        compiler_params=PARAMS,
    )(chip, parts)


def unpack(core, mine, other, width):
    n, rows, wide = mine.shape
    per_group = LANES // rows
    half = n * rows

    def kernel(core_ref, mine_ref, other_ref, weight_ref, bias_ref):
        for parts_ref, at in ((mine_ref, core_ref[0]), (other_ref, 1 - core_ref[0])):
            base = pl.multiple_of(at * half, half)
            for i in range(n):
                weight_ref[pl.ds(base + i * rows, rows), :] = parts_ref[i, :, :width].astype(F32)
            for g in range(n // per_group):
                line = parts_ref[g * per_group, :, width:].astype(F32)
                for i in range(1, per_group):
                    line = line + parts_ref[g * per_group + i, :, width:].astype(F32)
                line = jnp.sum(line, axis=0, keepdims=True)
                bias_ref[:, pl.ds(pl.multiple_of(base + g * LANES, LANES), LANES)] = line

    return pl.pallas_call(
        kernel,
        out_shape=(
            jax.ShapeDtypeStruct((2 * half, width), F32),
            jax.ShapeDtypeStruct((1, 2 * half), F32),
        ),
        in_specs=[IN_SMEM, IN_VMEM, IN_VMEM],
        out_specs=(IN_VMEM, IN_VMEM),
        compiler_params=PARAMS,
    )(core, mine, other)


def on_device(features, pick, tiles, coords, counts, weight, bias, cotangent):
    col_count = lax.axis_size("col")
    row_count = lax.axis_size("row")
    block_rows, width = features.shape
    slot_rows = block_rows // col_count
    exchange = functools.partial(lax.all_to_all, split_axis=0, concat_axis=0, tiled=True)

    def permute(x, step):
        pairs = []
        for col in range(col_count):
            turn = 1 - 2 * (col % 2)
            for row in range(row_count):
                target = (row + turn * step(turn * row % row_count)) % row_count
                pairs.append((col * row_count + row, col * row_count + target))
        return lax.ppermute(x, ("col", "row"), pairs)

    def swap(x, side, reach=1):
        return permute(x, lambda row: reach if row // reach % 2 == side else -reach)

    col, row = (lax.axis_index(axis).astype(jnp.int32) for axis in ("col", "row"))
    place = jnp.stack([row, 1 - 2 * lax.rem(col, 2)])

    bundles = bundle_tiles(place, counts, coords.reshape(-1), tiles[0])
    bundles = [bundles[0], swap(bundles[1], 0), swap(bundles[2], 1), swap(bundles[3], 0, 2)]
    sent = features[pick[0]].reshape(col_count, slot_rows, width)
    blocked = exchange(sent, "col").reshape(block_rows, width)

    blocks = [blocked] + [None] * (row_count - 1)
    ahead = behind = blocked
    for step in range(1, row_count // 2 + 1):
        ahead, behind = swap(behind, 0), swap(ahead, 1) if 2 * step < row_count else None
        if step == TIE:
            ahead, behind, *bundles = lax.optimization_barrier((ahead, behind, *bundles))
        blocks[step] = ahead
        if behind is not None:
            blocks[row_count - step] = behind

    sums = partial_sums(place, bundles, blocks)
    sums = [sums[0]] + [permute(sums[p], lambda _, p=p: p * STRIDE) for p in range(1, len(sums))]
    core = lax.rem(col, 2).reshape(1)
    hidden, keep, give = layer(core, sums, weight, bias.reshape(1, width), cotangent)

    chips = col_count // 2
    cores = [[2 * chip + k for chip in range(chips)] for k in range(2)]
    other_core = [(i, i ^ 1) for i in range(col_count)]
    parts = sum_two(keep, lax.ppermute(give, "col", other_core))
    parts = parts.reshape(chips, width // col_count, width + LANES)
    parts = exchange(parts, "col", axis_index_groups=cores)
    parts = exchange(sum_over_chips(parts, row_count), "row")
    parts = sum_over_row(lax.div(col, 2).reshape(1), parts, chips, width)
    mine = exchange(parts, "col", axis_index_groups=cores)
    other = lax.ppermute(mine, "col", other_core)
    weight_grad, bias_grad = unpack(core, mine, other, width)
    return hidden, weight_grad, bias_grad.reshape(width)


def solution(mesh):
    in_specs = (
        P(("col", "row"), None),
        P(("col", "row"), None),
        P(("col", "row"), None, None, None),
        P(("col", "row"), None, None),
        P(("col", "row")),
        P(),
        P(),
        P(("col", "row"), None),
    )
    out_specs = (P(("col", "row"), None), P(), P())
    return jax.shard_map(
        on_device, mesh=mesh, in_specs=in_specs, out_specs=out_specs, check_vma=False
    )
```

```python
import functools

import jax
import jax.numpy as jnp
from jax import lax
from jax.experimental import pallas as pl
from jax.experimental.pallas import tpu as pltpu
from jax.sharding import PartitionSpec as P

BF16 = jnp.bfloat16
F32 = jnp.float32
LANES = 128
META_ROWS = 16
STRIDE = 4
TIE = 1
VMEM_LIMIT = 16 * 1024 * 1024
IN_VMEM = pl.BlockSpec(memory_space=pltpu.VMEM)
IN_SMEM = pl.BlockSpec(memory_space=pltpu.SMEM)
IN_PLACE = pl.BlockSpec(memory_space=pl.ANY)
PARAMS = pltpu.CompilerParams(vmem_limit_bytes=VMEM_LIMIT)


def ring_place(place_ref, n):
    here, turn = place_ref[0], place_ref[1]
    near = jnp.where(lax.rem(here, 2) == 0, -1, 1)
    far = jnp.where(lax.rem(lax.div(here, 2) + lax.div(1 - turn, 2), 2) == 0, turn, -turn)
    return here, turn, near, far


def routes(near, far):
    return (0, near, -near, 2 * far)


def own_slot(output, first, n):
    return lax.rem(output - first + 3 * n, n)


def bundle_tiles(place, count, coords, tile_set):
    n, rows, columns = tile_set.shape
    size, groups = n // STRIDE, STRIDE - 1

    def kernel(place_ref, count_ref, coords_ref, tiles_ref, *refs):
        out_refs, (meta, tile_sems, meta_sems) = refs[:groups], refs[groups:]
        here, turn, near, far = ring_place(place_ref, n)
        copies = []
        for g, ahead in enumerate(routes(near, far)[1:]):
            for p in range(size):
                slot = own_slot(here + turn * (p * STRIDE + ahead), coords_ref[0], n)
                target = out_refs[g].at[p, pl.ds(0, rows)]
                sem = tile_sems.at[g * size + p]
                copies.append(pltpu.make_async_copy(tiles_ref.at[slot], target, sem))
                copies[-1].start()
                block = jnp.where(slot < count_ref[0], coords_ref[2 * slot + 1], -1)
                meta[g, p] = jnp.full(meta.shape[2:], block.astype(F32), F32).astype(BF16)
            notes = out_refs[g].at[:, pl.ds(rows, META_ROWS)]
            copies.append(pltpu.make_async_copy(meta.at[g], notes, meta_sems.at[g]))
            copies[-1].start()
        for copy in copies:
            copy.wait()

    bundle = jax.ShapeDtypeStruct((size, rows + META_ROWS, columns), tile_set.dtype)
    return pl.pallas_call(
        kernel,
        out_shape=[bundle] * groups,
        in_specs=[IN_SMEM] * 3 + [IN_PLACE],
        out_specs=[IN_PLACE] * groups,
        scratch_shapes=[
            pltpu.VMEM((groups, size, META_ROWS, columns), tile_set.dtype),
            pltpu.SemaphoreType.DMA((groups * size,)),
            pltpu.SemaphoreType.DMA((groups,)),
        ],
        compiler_params=PARAMS,
        cost_estimate=pl.CostEstimate(
            flops=0, bytes_accessed=2 * tile_set.size * 2, transcendentals=0
        ),
    )(place, count, coords, tile_set)


def partial_sum(place, count, coords, tile_set, bundles, blocks, p):
    groups, n = len(bundles), len(blocks)
    rows, width = blocks[0].shape

    def kernel(place_ref, count_ref, coords_ref, tiles_ref, *refs):
        bundle_refs, block_refs = refs[:groups], refs[groups : groups + n]
        out_ref, total, own, which, sem = refs[groups + n :]
        here, turn, near, _ = ring_place(place_ref, n)
        slot = own_slot(here + turn * p * STRIDE, coords_ref[0], n)
        fetch = pltpu.make_async_copy(tiles_ref.at[slot], own, sem)
        fetch.start()

        def away(block):
            return jnp.where(block < 0, -1, lax.rem(near * turn * (block - here) + n, n))

        which[0] = away(jnp.where(slot < count_ref[0], coords_ref[2 * slot + 1], -1))
        for g, bundle_ref in enumerate(bundle_refs):
            note = bundle_ref[p, rows : rows + META_ROWS, :LANES].astype(F32)
            which[1 + g] = away(jnp.max(note).astype(jnp.int32))
        total[...] = jnp.zeros_like(total)
        fetch.wait()
        for d, block_ref in enumerate(block_refs):
            for g in range(groups + 1):

                @pl.when(which[g] == d)
                def _():
                    tile = bundle_refs[g - 1][p, :rows, :] if g else own[...]
                    total[...] += jnp.dot(tile, block_ref[...], preferred_element_type=F32)

        out_ref[...] = total[...].astype(out_ref.dtype)

    return pl.pallas_call(
        kernel,
        out_shape=jax.ShapeDtypeStruct((rows, width), BF16 if p else F32),
        in_specs=[IN_SMEM] * 3 + [IN_PLACE] + [IN_VMEM] * (groups + n),
        out_specs=IN_VMEM,
        scratch_shapes=[
            pltpu.VMEM((rows, width), F32),
            pltpu.VMEM(tile_set.shape[1:], tile_set.dtype),
            pltpu.SMEM((groups + 1,), jnp.int32),
            pltpu.SemaphoreType.DMA,
        ],
        compiler_params=PARAMS,
        cost_estimate=pl.CostEstimate(
            flops=2 * (groups + 1) * rows * rows * width,
            bytes_accessed=4 * 1024 * 1024,
            transcendentals=0,
        ),
    )(place, count, coords, tile_set, *bundles, *blocks)


def layer(core, sums, weight, bias, cotangent):
    rows, width = cotangent.shape
    parts, half = len(sums), width // 2

    def kernel(core_ref, *refs):
        sum_refs = refs[:parts]
        weight_ref, bias_ref, cot_ref, hidden_ref, keep_ref, give_ref = refs[parts:]
        total = sum_refs[0][...].astype(F32)
        for sum_ref in sum_refs[1:]:
            total = total + sum_ref[...].astype(F32)
        aggregated = total.astype(BF16)
        pre = jnp.dot(aggregated, weight_ref[...], preferred_element_type=F32) + bias_ref[...]
        sig = jax.nn.sigmoid(pre)
        hidden_ref[...] = (pre * sig).astype(BF16)
        grad_pre = (cot_ref[...].astype(F32) * sig * (1.0 + pre * (1.0 - sig))).astype(BF16)
        over_nodes = (((0,), (0,)), ((), ()))
        ones = jnp.ones((rows, LANES), BF16)
        first = core_ref[0] == 0
        for out_ref, low in ((keep_ref, first), (give_ref, jnp.logical_not(first))):
            left = jnp.where(low, aggregated[:, :half], aggregated[:, half:])
            out_ref[:, :width] = lax.dot_general(
                left, grad_pre, over_nodes, preferred_element_type=F32
            ).astype(BF16)
            left = jnp.where(low, grad_pre[:, :half], grad_pre[:, half:])
            out_ref[:, width:] = lax.dot_general(
                left, ones, over_nodes, preferred_element_type=F32
            ).astype(BF16)

    gradient = jax.ShapeDtypeStruct((half, width + LANES), BF16)
    return pl.pallas_call(
        kernel,
        out_shape=(jax.ShapeDtypeStruct((rows, width), BF16), gradient, gradient),
        in_specs=[IN_SMEM] + [IN_VMEM] * (parts + 3),
        out_specs=(IN_VMEM, IN_VMEM, IN_VMEM),
        compiler_params=PARAMS,
        cost_estimate=pl.CostEstimate(
            flops=4 * rows * width * width,
            bytes_accessed=3 * 1024 * 1024,
            transcendentals=rows * width,
        ),
    )(core, *sums, weight, bias, cotangent)


def sum_two(left, right):
    def kernel(left_ref, right_ref, out_ref):
        out_ref[...] = (left_ref[...].astype(F32) + right_ref[...].astype(F32)).astype(BF16)

    return pl.pallas_call(
        kernel,
        out_shape=jax.ShapeDtypeStruct(left.shape, BF16),
        in_specs=[IN_VMEM] * 2,
        out_specs=IN_VMEM,
        compiler_params=PARAMS,
    )(left, right)


def sum_over_chips(parts, copies):
    n, rows, wide = parts.shape

    def kernel(parts_ref, out_ref):
        total = parts_ref[0].astype(F32)
        for i in range(1, n):
            total = total + parts_ref[i].astype(F32)
        packed = total.astype(BF16)
        for i in range(copies):
            out_ref[i] = packed

    return pl.pallas_call(
        kernel,
        out_shape=jax.ShapeDtypeStruct((copies, rows, wide), BF16),
        in_specs=[IN_VMEM],
        out_specs=IN_VMEM,
        compiler_params=PARAMS,
    )(parts)


def sum_over_row(chip, parts, copies, width):
    n, rows, wide = parts.shape

    def kernel(chip_ref, parts_ref, out_ref):
        total = parts_ref[0].astype(F32)
        for i in range(1, n):
            total = total + parts_ref[i].astype(F32)
        lane = lax.broadcasted_iota(jnp.int32, (rows, LANES), 1)
        row = lax.broadcasted_iota(jnp.int32, (rows, LANES), 0)
        mine = lane == lax.rem(chip_ref[0] * rows, LANES) + row
        tail = jnp.where(mine, total[:, width:], 0.0).astype(BF16)
        weights = total[:, :width].astype(BF16)
        for i in range(copies):
            out_ref[i, :, :width] = weights
            out_ref[i, :, width:] = tail

    return pl.pallas_call(
        kernel,
        out_shape=jax.ShapeDtypeStruct((copies, rows, wide), BF16),
        in_specs=[IN_SMEM, IN_VMEM],
        out_specs=IN_VMEM,
        compiler_params=PARAMS,
    )(chip, parts)


def unpack(core, mine, other, width):
    n, rows, wide = mine.shape
    per_group = LANES // rows
    half = n * rows

    def kernel(core_ref, mine_ref, other_ref, weight_ref, bias_ref):
        for parts_ref, at in ((mine_ref, core_ref[0]), (other_ref, 1 - core_ref[0])):
            base = pl.multiple_of(at * half, half)
            for i in range(n):
                weight_ref[pl.ds(base + i * rows, rows), :] = parts_ref[i, :, :width].astype(F32)
            for g in range(n // per_group):
                line = parts_ref[g * per_group, :, width:].astype(F32)
                for i in range(1, per_group):
                    line = line + parts_ref[g * per_group + i, :, width:].astype(F32)
                line = jnp.sum(line, axis=0, keepdims=True)
                bias_ref[:, pl.ds(pl.multiple_of(base + g * LANES, LANES), LANES)] = line

    return pl.pallas_call(
        kernel,
        out_shape=(
            jax.ShapeDtypeStruct((2 * half, width), F32),
            jax.ShapeDtypeStruct((1, 2 * half), F32),
        ),
        in_specs=[IN_SMEM, IN_VMEM, IN_VMEM],
        out_specs=(IN_VMEM, IN_VMEM),
        compiler_params=PARAMS,
    )(core, mine, other)


def on_device(features, pick, tiles, coords, counts, weight, bias, cotangent):
    col_count = lax.axis_size("col")
    row_count = lax.axis_size("row")
    block_rows, width = features.shape
    slot_rows = block_rows // col_count
    exchange = functools.partial(lax.all_to_all, split_axis=0, concat_axis=0, tiled=True)

    def permute(x, ahead):
        pairs = []
        for col in range(col_count):
            core = col % 2
            for row in range(row_count):
                target = (row + (1 - 2 * core) * ahead(core, row)) % row_count
                pairs.append((col * row_count + row, col * row_count + target))
        return lax.ppermute(x, ("col", "row"), pairs)

    def swap(x, side):
        return permute(x, lambda core, row: 1 if row % 2 != side else -1)

    def swap_far(x):
        return permute(x, lambda core, row: -2 if (row // 2 + core) % 2 ^ core else 2)

    col, row = (lax.axis_index(axis).astype(jnp.int32) for axis in ("col", "row"))
    place = jnp.stack([row, 1 - 2 * lax.rem(col, 2)])

    tile_list = (place, counts, coords.reshape(-1), tiles[0])
    bundles = bundle_tiles(*tile_list)
    bundles = [swap(bundles[0], 0), swap(bundles[1], 1), swap_far(bundles[2])]
    sent = features[pick[0]].reshape(col_count, slot_rows, width)
    blocked = exchange(sent, "col").reshape(block_rows, width)

    blocks = [blocked] + [None] * (row_count - 1)
    ahead = behind = blocked
    for step in range(1, row_count // 2 + 1):
        ahead, behind = swap(behind, 0), swap(ahead, 1) if 2 * step < row_count else None
        if step == TIE:
            ahead, behind, *bundles = lax.optimization_barrier((ahead, behind, *bundles))
        blocks[step] = ahead
        if behind is not None:
            blocks[row_count - step] = behind

    sums = [partial_sum(*tile_list, bundles, blocks, p) for p in range(row_count // STRIDE)]
    for p in range(1, len(sums)):
        sums[p] = permute(sums[p], lambda core, row, p=p: p * STRIDE)
    core = lax.rem(col, 2).reshape(1)
    hidden, keep, give = layer(core, sums, weight, bias.reshape(1, width), cotangent)

    chips = col_count // 2
    cores = [[2 * chip + k for chip in range(chips)] for k in range(2)]
    other_core = [(i, i ^ 1) for i in range(col_count)]
    parts = sum_two(keep, lax.ppermute(give, "col", other_core))
    parts = parts.reshape(chips, width // col_count, width + LANES)
    parts = exchange(parts, "col", axis_index_groups=cores)
    parts = exchange(sum_over_chips(parts, row_count), "row")
    parts = sum_over_row(lax.div(col, 2).reshape(1), parts, chips, width)
    mine = exchange(parts, "col", axis_index_groups=cores)
    other = lax.ppermute(mine, "col", other_core)
    weight_grad, bias_grad = unpack(core, mine, other, width)
    return hidden, weight_grad, bias_grad.reshape(width)


def solution(mesh):
    in_specs = (
        P(("col", "row"), None),
        P(("col", "row"), None),
        P(("col", "row"), None, None, None),
        P(("col", "row"), None, None),
        P(("col", "row")),
        P(),
        P(),
        P(("col", "row"), None),
    )
    out_specs = (P(("col", "row"), None), P(), P())
    return jax.shard_map(
        on_device, mesh=mesh, in_specs=in_specs, out_specs=out_specs, check_vma=False
    )
```

```python
import functools

import jax
import jax.numpy as jnp
from jax import lax
from jax.experimental import pallas as pl
from jax.experimental.pallas import tpu as pltpu
from jax.sharding import PartitionSpec as P

BF16 = jnp.bfloat16
F32 = jnp.float32
LANES = 128
META_ROWS = 16
STRIDE = 4
TIE = 1
VMEM_LIMIT = 16 * 1024 * 1024
IN_VMEM = pl.BlockSpec(memory_space=pltpu.VMEM)
IN_SMEM = pl.BlockSpec(memory_space=pltpu.SMEM)
IN_PLACE = pl.BlockSpec(memory_space=pl.ANY)
PARAMS = pltpu.CompilerParams(vmem_limit_bytes=VMEM_LIMIT)


def ring_place(place_ref, n):
    here, turn = place_ref[0], place_ref[1]
    near = jnp.where(lax.rem(here, 2) == 0, -1, 1)
    far = jnp.where(lax.rem(lax.div(here, 2) + lax.div(1 - turn, 2), 2) == 0, turn, -turn)
    return here, turn, near, far


def routes(near, far):
    return (0, near, -near, 2 * far)


def own_slot(output, first, n):
    return lax.rem(output - first + 3 * n, n)


def bundle_tiles(place, count, coords, tile_set):
    n, rows, columns = tile_set.shape
    size, groups = n // STRIDE, STRIDE - 1

    def kernel(place_ref, count_ref, coords_ref, tiles_ref, *refs):
        out_refs, (meta, tile_sems, meta_sems) = refs[:groups], refs[groups:]
        here, turn, near, far = ring_place(place_ref, n)
        copies = []
        for g, ahead in enumerate(routes(near, far)[1:]):
            for p in range(size):
                slot = own_slot(here + turn * (p * STRIDE + ahead), coords_ref[0], n)
                target = out_refs[g].at[p, pl.ds(0, rows)]
                sem = tile_sems.at[g * size + p]
                copies.append(pltpu.make_async_copy(tiles_ref.at[slot], target, sem))
                copies[-1].start()
                block = jnp.where(slot < count_ref[0], coords_ref[2 * slot + 1], -1)
                meta[g, p] = jnp.full(meta.shape[2:], block.astype(F32), F32).astype(BF16)
            notes = out_refs[g].at[:, pl.ds(rows, META_ROWS)]
            copies.append(pltpu.make_async_copy(meta.at[g], notes, meta_sems.at[g]))
            copies[-1].start()
        for copy in copies:
            copy.wait()

    bundle = jax.ShapeDtypeStruct((size, rows + META_ROWS, columns), tile_set.dtype)
    return pl.pallas_call(
        kernel,
        out_shape=[bundle] * groups,
        in_specs=[IN_SMEM] * 3 + [IN_PLACE],
        out_specs=[IN_PLACE] * groups,
        scratch_shapes=[
            pltpu.VMEM((groups, size, META_ROWS, columns), tile_set.dtype),
            pltpu.SemaphoreType.DMA((groups * size,)),
            pltpu.SemaphoreType.DMA((groups,)),
        ],
        compiler_params=PARAMS,
        cost_estimate=pl.CostEstimate(
            flops=0, bytes_accessed=2 * tile_set.size * 2, transcendentals=0
        ),
    )(place, count, coords, tile_set)


def partial_sum(place, count, coords, tile_set, bundles, blocks, p):
    groups, n = len(bundles), len(blocks)
    rows, width = blocks[0].shape

    def kernel(place_ref, count_ref, coords_ref, tiles_ref, *refs):
        bundle_refs, block_refs = refs[:groups], refs[groups : groups + n]
        out_ref, total, own, which, sem = refs[groups + n :]
        here, turn, near, _ = ring_place(place_ref, n)
        slot = own_slot(here + turn * p * STRIDE, coords_ref[0], n)
        fetch = pltpu.make_async_copy(tiles_ref.at[slot], own, sem)
        fetch.start()

        def away(block):
            return jnp.where(block < 0, -1, lax.rem(near * turn * (block - here) + n, n))

        which[0] = away(jnp.where(slot < count_ref[0], coords_ref[2 * slot + 1], -1))
        for g, bundle_ref in enumerate(bundle_refs):
            note = bundle_ref[p, rows : rows + META_ROWS, :LANES].astype(F32)
            which[1 + g] = away(jnp.max(note).astype(jnp.int32))
        total[...] = jnp.zeros_like(total)
        fetch.wait()
        for d, block_ref in enumerate(block_refs):
            for g in range(groups + 1):

                @pl.when(which[g] == d)
                def _():
                    tile = bundle_refs[g - 1][p, :rows, :] if g else own[...]
                    total[...] += jnp.dot(tile, block_ref[...], preferred_element_type=F32)

        out_ref[...] = total[...].astype(out_ref.dtype)

    return pl.pallas_call(
        kernel,
        out_shape=jax.ShapeDtypeStruct((rows, width), BF16 if p else F32),
        in_specs=[IN_SMEM] * 3 + [IN_PLACE] + [IN_VMEM] * (groups + n),
        out_specs=IN_VMEM,
        scratch_shapes=[
            pltpu.VMEM((rows, width), F32),
            pltpu.VMEM(tile_set.shape[1:], tile_set.dtype),
            pltpu.SMEM((groups + 1,), jnp.int32),
            pltpu.SemaphoreType.DMA,
        ],
        compiler_params=PARAMS,
        cost_estimate=pl.CostEstimate(
            flops=2 * (groups + 1) * rows * rows * width,
            bytes_accessed=4 * 1024 * 1024,
            transcendentals=0,
        ),
    )(place, count, coords, tile_set, *bundles, *blocks)


def gradient_half(low, left, grad_pre, out_ref):
    rows, width = grad_pre.shape
    half = width // 2
    over_nodes = (((0,), (0,)), ((), ()))
    mine = jnp.where(low, left[:, :half], left[:, half:])
    out_ref[:, :width] = lax.dot_general(
        mine, grad_pre, over_nodes, preferred_element_type=F32
    ).astype(BF16)
    mine = jnp.where(low, grad_pre[:, :half], grad_pre[:, half:])
    ones = jnp.ones((rows, LANES), BF16)
    out_ref[:, width:] = lax.dot_general(
        mine, ones, over_nodes, preferred_element_type=F32
    ).astype(BF16)


def layer(core, sums, weight, bias, cotangent):
    rows, width = cotangent.shape
    parts = len(sums)

    def kernel(core_ref, *refs):
        sum_refs = refs[:parts]
        weight_ref, bias_ref, cot_ref, hidden_ref, agg_ref, grad_ref, give_ref = refs[parts:]
        total = sum_refs[0][...].astype(F32)
        for sum_ref in sum_refs[1:]:
            total = total + sum_ref[...].astype(F32)
        aggregated = total.astype(BF16)
        pre = jnp.dot(aggregated, weight_ref[...], preferred_element_type=F32) + bias_ref[...]
        sig = jax.nn.sigmoid(pre)
        hidden_ref[...] = (pre * sig).astype(BF16)
        grad_pre = (cot_ref[...].astype(F32) * sig * (1.0 + pre * (1.0 - sig))).astype(BF16)
        agg_ref[...] = aggregated
        grad_ref[...] = grad_pre
        gradient_half(core_ref[0] != 0, aggregated, grad_pre, give_ref)

    nodes = jax.ShapeDtypeStruct((rows, width), BF16)
    return pl.pallas_call(
        kernel,
        out_shape=(nodes, nodes, nodes, jax.ShapeDtypeStruct((width // 2, width + LANES), BF16)),
        in_specs=[IN_SMEM] + [IN_VMEM] * (parts + 3),
        out_specs=(IN_VMEM,) * 4,
        compiler_params=PARAMS,
        cost_estimate=pl.CostEstimate(
            flops=3 * rows * width * width,
            bytes_accessed=3 * 1024 * 1024,
            transcendentals=rows * width,
        ),
    )(core, *sums, weight, bias, cotangent)


def own_half(core, aggregated, grad_pre):
    rows, width = grad_pre.shape

    def kernel(core_ref, agg_ref, grad_ref, keep_ref):
        gradient_half(core_ref[0] == 0, agg_ref[...], grad_ref[...], keep_ref)

    return pl.pallas_call(
        kernel,
        out_shape=jax.ShapeDtypeStruct((width // 2, width + LANES), BF16),
        in_specs=[IN_SMEM, IN_VMEM, IN_VMEM],
        out_specs=IN_VMEM,
        compiler_params=PARAMS,
        cost_estimate=pl.CostEstimate(
            flops=rows * width * width, bytes_accessed=1024 * 1024, transcendentals=0
        ),
    )(core, aggregated, grad_pre)


def sum_two(left, right):
    def kernel(left_ref, right_ref, out_ref):
        out_ref[...] = (left_ref[...].astype(F32) + right_ref[...].astype(F32)).astype(BF16)

    return pl.pallas_call(
        kernel,
        out_shape=jax.ShapeDtypeStruct(left.shape, BF16),
        in_specs=[IN_VMEM] * 2,
        out_specs=IN_VMEM,
        compiler_params=PARAMS,
    )(left, right)


def sum_over_chips(parts, copies):
    n, rows, wide = parts.shape

    def kernel(parts_ref, out_ref):
        total = parts_ref[0].astype(F32)
        for i in range(1, n):
            total = total + parts_ref[i].astype(F32)
        packed = total.astype(BF16)
        for i in range(copies):
            out_ref[i] = packed

    return pl.pallas_call(
        kernel,
        out_shape=jax.ShapeDtypeStruct((copies, rows, wide), BF16),
        in_specs=[IN_VMEM],
        out_specs=IN_VMEM,
        compiler_params=PARAMS,
    )(parts)


def sum_over_row(chip, parts, copies, width):
    n, rows, wide = parts.shape

    def kernel(chip_ref, parts_ref, out_ref):
        total = parts_ref[0].astype(F32)
        for i in range(1, n):
            total = total + parts_ref[i].astype(F32)
        lane = lax.broadcasted_iota(jnp.int32, (rows, LANES), 1)
        row = lax.broadcasted_iota(jnp.int32, (rows, LANES), 0)
        mine = lane == lax.rem(chip_ref[0] * rows, LANES) + row
        tail = jnp.where(mine, total[:, width:], 0.0).astype(BF16)
        weights = total[:, :width].astype(BF16)
        for i in range(copies):
            out_ref[i, :, :width] = weights
            out_ref[i, :, width:] = tail

    return pl.pallas_call(
        kernel,
        out_shape=jax.ShapeDtypeStruct((copies, rows, wide), BF16),
        in_specs=[IN_SMEM, IN_VMEM],
        out_specs=IN_VMEM,
        compiler_params=PARAMS,
    )(chip, parts)


def unpack(core, mine, other, width):
    n, rows, wide = mine.shape
    per_group = LANES // rows
    half = n * rows

    def kernel(core_ref, mine_ref, other_ref, weight_ref, bias_ref):
        for parts_ref, at in ((mine_ref, core_ref[0]), (other_ref, 1 - core_ref[0])):
            base = pl.multiple_of(at * half, half)
            for i in range(n):
                weight_ref[pl.ds(base + i * rows, rows), :] = parts_ref[i, :, :width].astype(F32)
            for g in range(n // per_group):
                line = parts_ref[g * per_group, :, width:].astype(F32)
                for i in range(1, per_group):
                    line = line + parts_ref[g * per_group + i, :, width:].astype(F32)
                line = jnp.sum(line, axis=0, keepdims=True)
                bias_ref[:, pl.ds(pl.multiple_of(base + g * LANES, LANES), LANES)] = line

    return pl.pallas_call(
        kernel,
        out_shape=(
            jax.ShapeDtypeStruct((2 * half, width), F32),
            jax.ShapeDtypeStruct((1, 2 * half), F32),
        ),
        in_specs=[IN_SMEM, IN_VMEM, IN_VMEM],
        out_specs=(IN_VMEM, IN_VMEM),
        compiler_params=PARAMS,
    )(core, mine, other)


def on_device(features, pick, tiles, coords, counts, weight, bias, cotangent):
    col_count = lax.axis_size("col")
    row_count = lax.axis_size("row")
    block_rows, width = features.shape
    slot_rows = block_rows // col_count
    exchange = functools.partial(lax.all_to_all, split_axis=0, concat_axis=0, tiled=True)

    def permute(x, ahead):
        pairs = []
        for col in range(col_count):
            core = col % 2
            for row in range(row_count):
                target = (row + (1 - 2 * core) * ahead(core, row)) % row_count
                pairs.append((col * row_count + row, col * row_count + target))
        return lax.ppermute(x, ("col", "row"), pairs)

    def swap(x, side):
        return permute(x, lambda core, row: 1 if row % 2 != side else -1)

    def swap_far(x):
        return permute(x, lambda core, row: -2 if (row // 2 + core) % 2 ^ core else 2)

    col, row = (lax.axis_index(axis).astype(jnp.int32) for axis in ("col", "row"))
    place = jnp.stack([row, 1 - 2 * lax.rem(col, 2)])

    tile_list = (place, counts, coords.reshape(-1), tiles[0])
    bundles = bundle_tiles(*tile_list)
    bundles = [swap(bundles[0], 0), swap(bundles[1], 1), swap_far(bundles[2])]
    sent = features[pick[0]].reshape(col_count, slot_rows, width)
    blocked = exchange(sent, "col").reshape(block_rows, width)

    blocks = [blocked] + [None] * (row_count - 1)
    ahead = behind = blocked
    for step in range(1, row_count // 2 + 1):
        ahead, behind = swap(behind, 0), swap(ahead, 1) if 2 * step < row_count else None
        if step == TIE:
            ahead, behind, *bundles = lax.optimization_barrier((ahead, behind, *bundles))
        blocks[step] = ahead
        if behind is not None:
            blocks[row_count - step] = behind

    sums = [partial_sum(*tile_list, bundles, blocks, p) for p in range(row_count // STRIDE)]
    for p in range(1, len(sums)):
        sums[p] = permute(sums[p], lambda core, row, p=p: p * STRIDE)
    core = lax.rem(col, 2).reshape(1)
    hidden, aggregated, grad_pre, give = layer(
        core, sums, weight, bias.reshape(1, width), cotangent
    )
    keep = own_half(core, aggregated, grad_pre)

    chips = col_count // 2
    cores = [[2 * chip + k for chip in range(chips)] for k in range(2)]
    other_core = [(i, i ^ 1) for i in range(col_count)]
    parts = sum_two(keep, lax.ppermute(give, "col", other_core))
    parts = parts.reshape(chips, width // col_count, width + LANES)
    parts = exchange(parts, "col", axis_index_groups=cores)
    parts = exchange(sum_over_chips(parts, row_count), "row")
    parts = sum_over_row(lax.div(col, 2).reshape(1), parts, chips, width)
    mine = exchange(parts, "col", axis_index_groups=cores)
    other = lax.ppermute(mine, "col", other_core)
    weight_grad, bias_grad = unpack(core, mine, other, width)
    return hidden, weight_grad, bias_grad.reshape(width)


def solution(mesh):
    in_specs = (
        P(("col", "row"), None),
        P(("col", "row"), None),
        P(("col", "row"), None, None, None),
        P(("col", "row"), None, None),
        P(("col", "row")),
        P(),
        P(),
        P(("col", "row"), None),
    )
    out_specs = (P(("col", "row"), None), P(), P())
    return jax.shard_map(
        on_device, mesh=mesh, in_specs=in_specs, out_specs=out_specs, check_vma=False
    )
```
